128 devices in a mesh: wt: 2 (over y_hi), ctx: 64 (over y_lo, z, x, core).
Axes of the slice: x: 4, y: 4 (y_hi: 2, y_lo: 2; y = y_hi * 2 + y_lo), z: 4, core: 2. Of those that a mesh axis runs over, the one named last changes fastest.
Arguments:
- tokens: bfloat16 [2, 8192, 896], P('wt', 'ctx'), may hold values from -6 to 6
- cotangent: bfloat16 [2, 8192, 896], P('wt', 'ctx'), may hold values from -6 to 6
- block_pair: int32 [2, 64], P('wt'), may hold values from 0 to 63, as said below
- first_gain: bfloat16 [896], P('wt'), may hold values from 0.5 to 1.5
- query_weight: bfloat16 [896, 896], P('wt'), may hold values from -0.25 to 0.25
- query_bias: bfloat16 [896], P('wt'), may hold values from -3 to 3
- key_weight: bfloat16 [896, 128], P('wt'), may hold values from -0.25 to 0.25
- key_bias: bfloat16 [128], P('wt'), may hold values from -3 to 3
- value_weight: bfloat16 [896, 128], P('wt'), may hold values from -0.1875 to 0.1875
- value_bias: bfloat16 [128], P('wt'), may hold values from -3 to 3
- output_weight: bfloat16 [896, 896], P('wt'), may hold values from -0.75 to 0.75
- second_gain: bfloat16 [896], P('wt'), may hold values from 0.5 to 1.5
- gate_weight: bfloat16 [896, 4864], P('wt'), may hold values from -0.1875 to 0.1875
- up_weight: bfloat16 [896, 4864], P('wt'), may hold values from -0.1875 to 0.1875
- down_weight: bfloat16 [4864, 896], P('wt'), may hold values from -0.078125 to 0.078125
Outputs:
- layer_out: bfloat16 [2, 8192, 896], P('wt', 'ctx')
- input_grad: float32 [2, 8192, 896], P('wt', 'ctx')
- first_gain_grad: float32 [896], P('wt')
- query_weight_grad: float32 [896, 896], P('wt')
- query_bias_grad: float32 [896], P('wt')
- key_weight_grad: float32 [896, 128], P('wt')
- key_bias_grad: float32 [128], P('wt')
- value_weight_grad: float32 [896, 128], P('wt')
- value_bias_grad: float32 [128], P('wt')
- output_weight_grad: float32 [896, 896], P('wt')
- second_gain_grad: float32 [896], P('wt')
- gate_weight_grad: float32 [896, 4864], P('wt')
- up_weight_grad: float32 [896, 4864], P('wt')
- down_weight_grad: float32 [4864, 896], P('wt')
The draws below stay inside these ranges and needn't reach their ends.
Inputs may be any that keep to these rules, and one draw needn't show every extreme that they name: Each row is a permutation of the numbers 0 to 63; device slot i holds the causal blocks block_pair[s, i] and 127 - block_pair[s, i].
All inputs are finite; a program needn't handle non-finite values.
Results may differ from the reference program's by a relative error of at most 0.03.
Values may be sent and summed in bfloat16 or wider, within the bound.
No kernel may reach another device: no remote copies, remote signals or barrier semaphores. Data moves between devices by JAX's collectives and lax.ppermute only.
A program may use at most 256 MiB of HBM per device.

```python
import math
import jax
import jax.numpy as jnp
from jax import lax

D = 896
FF = 4864
HEADS = 14
KVH = 2
HD = 64
TOK_DEV = 128
PAIRS = 64
SEQS = 2
SEQ_LEN = 8192


def shuffle_row(one_key):
    return jax.random.permutation(one_key, PAIRS)


def draw_block_pair(key, part):
    key = jax.random.fold_in(key, 7)
    keys = jax.random.split(key, SEQS)
    return jax.vmap(shuffle_row)(keys).astype(jnp.int32)


def block_scale(stream_key, dims, shards, smallest, largest):
    level = 1.0
    for dim, parts in shards:
        heights = jax.random.uniform(jax.random.fold_in(jax.random.fold_in(stream_key, 6), dim), (parts,), jnp.float32, smallest / len(shards), largest / len(shards))
        level = level * jnp.repeat(jnp.exp(heights), dims[dim] // parts).reshape((-1,) + (1,) * (len(dims) - 1 - dim))
    return level


def gaussian(stream_key, extent, width, limit, shards=(), kind=jnp.bfloat16):
    level = block_scale(stream_key, extent, shards, -0.22, 0.18) if shards else 1.0
    entries = jax.random.normal(stream_key, extent, jnp.float32) * width * level
    return jnp.minimum(jnp.maximum(entries, -limit), limit).astype(kind)


def setup_inputs(seed: int = 0) -> dict:
    key_of = jax.random.split(jax.random.key(seed), 16)
    return {
        "tokens": gaussian(key_of[0], (SEQS, SEQ_LEN, D), 1.0, 6.0, ((0, 2), (1, 64))),
        "cotangent": gaussian(key_of[1], (SEQS, SEQ_LEN, D), 1.0, 6.0, ((0, 2), (1, 64))),
        "block_pair": draw_block_pair(jax.random.fold_in(key_of[15], 71), 0),
        "first_gain": jnp.clip(1.0 + 0.1 * jax.random.normal(key_of[3], (D,), jnp.float32), 0.5, 1.5).astype(jnp.bfloat16),
        "query_weight": gaussian(key_of[4], (D, HEADS * HD), (D // 2) ** -0.5, 0.25, ((0, 2),)),
        "query_bias": gaussian(key_of[5], (HEADS * HD,), 0.5, 3.0, ((0, 2),)),
        "key_weight": gaussian(key_of[6], (D, KVH * HD), (D // 2) ** -0.5, 0.25, ((0, 2),)),
        "key_bias": gaussian(key_of[7], (KVH * HD,), 0.5, 3.0, ((0, 2),)),
        "value_weight": gaussian(key_of[8], (D, KVH * HD), D ** -0.5, 0.1875, ((0, 2),)),
        "value_bias": gaussian(key_of[9], (KVH * HD,), 0.5, 3.0, ((0, 2),)),
        "output_weight": gaussian(key_of[10], (HEADS * HD, D), (HEADS * HD // 16) ** -0.5, 0.75, ((0, 2),)),
        "second_gain": jnp.clip(1.0 + 0.1 * jax.random.normal(key_of[11], (D,), jnp.float32), 0.5, 1.5).astype(jnp.bfloat16),
        "gate_weight": gaussian(key_of[12], (D, FF), D ** -0.5, 0.1875, ((0, 2),)),
        "up_weight": gaussian(key_of[13], (D, FF), D ** -0.5, 0.1875, ((0, 2),)),
        "down_weight": gaussian(key_of[14], (FF, D), FF ** -0.5, 0.078125, ((0, 2),)),
    }


THETA = 1000000.0
EPS = 1e-06
MASKED = -1e+30
HIGH = lax.Precision.HIGHEST

@jax.custom_vjp
def low(v):
    return lax.optimization_barrier(v.astype(jnp.bfloat16)).astype(jnp.float32)

@jax.custom_vjp
def low_back(v):
    return v

def low_keep(v):
    return (low(v), None)

def low_pass(kept, grad):
    return (grad,)

def back_keep(v):
    return (v, None)

def back_low(kept, grad):
    return (low(grad),)
low.defvjp(low_keep, low_pass)
low_back.defvjp(back_keep, back_low)

def positions_of(pairs):
    half = TOK_DEV // 2
    offsets = jnp.arange(half, dtype=jnp.int32)
    first = pairs[:, None] * half + offsets[None, :]
    second = (2 * PAIRS - 1 - pairs)[:, None] * half + offsets[None, :]
    return jnp.concatenate([first, second], axis=1).reshape(-1).astype(jnp.int32)

def rotary(places, sign):
    count = HD // 2
    inverse = THETA ** (-(2.0 * jnp.arange(count, dtype=jnp.float32)) / HD)
    angle = places.astype(jnp.float32)[:, None] * inverse[None, :]
    cosine = jnp.cos(angle)
    sine = jnp.sin(angle) * sign
    return (jnp.concatenate([cosine, cosine], 1), jnp.concatenate([sine, sine], 1))

def rotate(values, cosine, sine):
    half = values.shape[-1] // 2
    turned = jnp.concatenate([-values[..., half:], values[..., :half]], -1)
    return values * cosine[:, None, :] + turned * sine[:, None, :]

def rms(values, gain):
    scale = lax.rsqrt(lax.optimization_barrier(jnp.mean(values * values, axis=-1, keepdims=True)) + EPS)
    return values * scale * gain

def attention(queries, keys, values, places):
    length = queries.shape[0]
    block = math.gcd(512, length)
    group = HEADS // KVH
    query_blocks = queries.reshape(length // block, block, KVH, group, HD)
    place_blocks = places.reshape(length // block, block)

    def one_block(inputs):
        query_part, query_place = inputs
        raw = low_back(jnp.einsum('tkgd,skd->kgts', query_part, keys, precision=HIGH))
        scores = raw * HD ** (-0.5)
        allowed = places[None, :] <= query_place[:, None]
        scores = jnp.where(allowed[None, None], scores, MASKED)
        total = jax.nn.logsumexp(scores, axis=-1, keepdims=True)
        probs = low(jnp.exp(scores - total))
        return jnp.einsum('kgts,skd->tkgd', probs, values, precision=HIGH)
    result = lax.map(jax.checkpoint(one_block), (query_blocks, place_blocks))
    return result.reshape(length, HEADS * HD)

def layer(inputs, first_gain, query_weight, query_bias, key_weight, key_bias, value_weight, value_bias, output_weight, second_gain, gate_weight, up_weight, down_weight, places_all):
    length = TOK_DEV * PAIRS
    results = []
    for seq in range(SEQS):
        source = inputs[seq]
        places = places_all[seq]
        normed_one = low(rms(source, first_gain))
        query_pre = low_back(jnp.dot(normed_one, query_weight, precision=HIGH) + query_bias)
        key_pre = low_back(jnp.dot(normed_one, key_weight, precision=HIGH) + key_bias)
        value_pre = low(low_back(jnp.dot(normed_one, value_weight, precision=HIGH) + value_bias))
        cosine, sine = rotary(places, 1.0)
        queries = low(rotate(query_pre.reshape(length, HEADS, HD), cosine, sine))
        keys = low(rotate(key_pre.reshape(length, KVH, HD), cosine, sine))
        values = value_pre.reshape(length, KVH, HD)
        attended = low(low_back(attention(queries, keys, values, places)))
        middle = source + low_back(jnp.dot(attended, output_weight, precision=HIGH))
        normed_two = low(rms(middle, second_gain))
        gate = low_back(jnp.dot(normed_two, gate_weight, precision=HIGH))
        upper = low_back(jnp.dot(normed_two, up_weight, precision=HIGH))
        hidden = low(jax.nn.silu(gate) * upper)
        results.append(middle + low_back(jnp.dot(hidden, down_weight, precision=HIGH)))
    return jnp.stack(results)

def reference(tokens, cotangent, block_pair, first_gain, query_weight, query_bias, key_weight, key_bias, value_weight, value_bias, output_weight, second_gain, gate_weight, up_weight, down_weight):
    places_all = jnp.stack([positions_of(block_pair[seq]) for seq in range(SEQS)])
    floats = tuple((item.astype(jnp.float32) for item in (tokens, first_gain, query_weight, query_bias, key_weight, key_bias, value_weight, value_bias, output_weight, second_gain, gate_weight, up_weight, down_weight)))

    def forward(*items):
        return layer(*items, places_all)
    result, pullback = jax.vjp(forward, *floats)
    grads = pullback(cotangent.astype(jnp.float32))
    return (result.astype(jnp.bfloat16), grads[0], grads[1], grads[2], grads[3], grads[4], grads[5], grads[6], grads[7], grads[8], grads[9], grads[10], grads[11], grads[12])
```

```python
import functools

import jax
import jax.numpy as jnp
from jax import lax
from jax.experimental import pallas as pl
from jax.experimental.pallas import tpu as pltpu
from jax.sharding import Mesh
from jax.sharding import PartitionSpec as P

HD = 64
THETA = 1000000.0
EPS = 1e-06
MASKED = -1e30
D = 896
FF = 4864
HEADS = 14
TOK = 128
SEQ = 8192
TILE = 512
BLOCKS = TILE // 64
AB, BA = (1, 3), (3, 1)
GRAY_AB, GRAY_BA = (0, 1, 3, 2), (0, 3, 1, 2)
FHALF = FF // 2
FS = 640
ROWS = 448
bf16 = jnp.bfloat16
f32 = jnp.float32


def dot(a, b):
    return jnp.dot(a, b, preferred_element_type=f32)


def dot_nt(a, b):
    return lax.dot_general(a, b, (((1,), (1,)), ((), ())), preferred_element_type=f32)


def dot_tn(a, b):
    return lax.dot_general(a, b, (((0,), (0,)), ((), ())), preferred_element_type=f32)


def shift(a, axis, s):
    return lax.ppermute(a, axis, [(i, (i + s) % 4) for i in range(4)])


def swap_heads(a):
    parts = []
    for i in range(HEADS // 2):
        t = a[:, 128 * i : 128 * (i + 1)].T
        parts.append(jnp.concatenate([t[:64], t[64:]], axis=1))
    return jnp.concatenate(parts, axis=1)


def rope(v, cosine, sine):
    lane = lax.broadcasted_iota(jnp.int32, v.shape, 1)
    turned = jnp.where(lane % 64 < 32, pltpu.roll(v, 96, 1), pltpu.roll(v, 32, 1))
    return v * cosine + turned * sine


def two_groups(a):
    lane = lax.broadcasted_iota(jnp.int32, a.shape, 1)
    zero = jnp.zeros_like(a)
    return jnp.concatenate(
        [jnp.where(lane < ROWS, a, zero), jnp.where(lane < ROWS, zero, a)], axis=0
    )


def one_group(a):
    lane = lax.broadcasted_iota(jnp.int32, (64, D), 1)
    return jnp.where(lane < ROWS, a[0:64], a[64:128])


def pack_first_kernel(ids, k, v, g1, g2, qb, kb, vb, out):
    at = pl.ds(pl.multiple_of(ids[4] * 224, 32), 224)
    out[0:224, 0:128] = k[at, :]
    out[0:224, 128:256] = v[at, :]

    def lines(ref):
        row = ref[...].astype(f32).reshape(1, ROWS)
        return [row[:, 0:256], jnp.concatenate([row[:, 256:], jnp.zeros((1, 64), f32)], axis=1)]

    last = [r[...].astype(f32).reshape(1, 64) for r in (kb, vb)]
    last = jnp.concatenate(last + [jnp.zeros((1, 128), f32)], axis=1)
    rows = lines(g1) + lines(g2) + lines(qb) + [last, jnp.zeros((9, 256), f32)]
    out[224:240, :] = jnp.concatenate(rows, axis=0).astype(bf16)


def pack_qo_kernel(ids, wo, wq, out, sems):
    rows = pl.ds(pl.multiple_of(ids[4] * 224, 32), 224)
    made = [
        pltpu.make_async_copy(wq.at[rows, :], out.at[0:224, :], sems.at[0]),
        pltpu.make_async_copy(wo.at[rows, :], out.at[224:448, :], sems.at[1]),
    ]
    for m in made:
        m.start()
    for m in made:
        m.wait()


def pack_feed_kernel(ids, gate, up, down, send, own, dn, sems):
    wt, member = ids[0], ids[5]

    def copies(width):
        moves = []
        for dst, half in ((own, wt), (send, 1 - wt)):
            at = pl.ds(pl.multiple_of(half * FHALF + member * FS, 128), width)
            moves.append((gate.at[:, at], dst.at[:, 0:width]))
            moves.append((up.at[:, at], dst.at[:, FS : FS + width]))
        rows = pl.ds(pl.multiple_of(member * FS, 128), width)
        moves.append((down.at[rows, :], dn.at[0:width, :]))
        made = [pltpu.make_async_copy(a, b, sems.at[i]) for i, (a, b) in enumerate(moves)]
        for m in made:
            m.start()
        for m in made:
            m.wait()

    @pl.when(member < 3)
    def _():
        copies(FS)

    @pl.when(member == 3)
    def _():
        copies(512)
        for dst in (own, send):
            dst[:, 512:FS] = jnp.zeros((ROWS, FS - 512), bf16)
            dst[:, FS + 512 :] = jnp.zeros((ROWS, FS - 512), bf16)
        dn[512:, :] = jnp.zeros((FS - 512, D), bf16)


def parts_of(ids):
    wt, core = ids[0], ids[4]
    mine = pl.ds(pl.multiple_of(wt * ROWS, 64), ROWS)
    near = pl.ds(pl.multiple_of((1 - wt) * ROWS + core * 224, 32), 224)
    far = pl.ds(pl.multiple_of((1 - wt) * ROWS + (1 - core) * 224, 32), 224)
    return mine, near, far


def project_kernel(
    ids, tok, k, v, g1, g2, qb, kb, vb, got, got2, cos, sin, w, gains, n1_ref, kv_ref
):
    wt = ids[0]
    mine, near, far = parts_of(ids)
    w[mine, 0:128] = k[...]
    w[mine, 128:256] = v[...]
    w[near, :] = got[0:224, :]
    w[far, :] = got2[0:224, :]
    other = got[224:240, :].astype(f32)

    def whole(own, theirs):
        own = own[...].astype(f32).reshape(1, theirs.shape[1])
        first = jnp.concatenate([own, theirs], axis=1)
        second = jnp.concatenate([theirs, own], axis=1)
        return jnp.where(wt == 0, first, second)

    def long(at):
        return jnp.concatenate([other[at : at + 1, :], other[at + 1 : at + 2, 0:192]], axis=1)

    gain = whole(g1, long(0))
    bias = jnp.concatenate(
        [whole(kb, other[6:7, 0:64]), whole(vb, other[6:7, 64:128])], axis=1
    )
    gains[...] = jnp.concatenate(
        [gain, whole(g2, long(2)), whole(qb, long(4)), jnp.zeros((5, D), f32)], axis=0
    )
    x = tok[...].astype(f32)
    r = lax.rsqrt(jnp.mean(x * x, axis=-1, keepdims=True) + EPS)
    n1 = (x * r * gain).astype(bf16)
    n1_ref[...] = n1
    pre = dot(n1, w[...]) + bias
    kv_ref[:, 0:128] = rope(pre[:, 0:128], cos[...], sin[...]).astype(bf16)
    kv_ref[:, 128:256] = pre[:, 128:256].astype(bf16)


def tile_mask(scores, block, tile):
    row = lax.broadcasted_iota(jnp.int32, scores.shape, 0)
    lane = lax.broadcasted_iota(jnp.int32, scores.shape, 1)
    return jnp.where(row - lane % 64 <= block * 64 - tile * TILE, scores, MASKED)


def over_tiles(own, step):
    high = 2 * 64 - 1 - own
    low_full = own // BLOCKS
    high_full = high // BLOCKS

    def body(i, carry):
        late = (i >= low_full).astype(jnp.int32)
        step(late, i - late * low_full, None)
        return carry

    lax.fori_loop(0, low_full + high_full, body, 0)
    step(0, low_full, own)
    step(1, high_full, high)


def attend_kernel(ids, table, n1, wq, wo, got, got2, cos, sin, x, gains, *rest):
    pieces = rest[:4]
    kv_out, qt, ot_ref, lse_ref, att_ref, mid_ref, n2_ref, wq_out, wo_out = rest[4:13]
    qbd, acc, top, kv, wq_ref, wo_ref, sems = rest[13:]
    mine, near, far = parts_of(ids)
    for ref, own_part, at in ((wq_ref, wq, 0), (wo_ref, wo, 224)):
        ref[mine, :] = own_part[...]
        ref[near, :] = got[at : at + 224, :]
        ref[far, :] = got2[at : at + 224, :]
    pre = dot(n1[...], wq_ref[...]) + gains[2:3, :]
    q = [
        rope(pre[:, 128 * i : 128 * (i + 1)], cos[...], sin[...]).astype(bf16).astype(f32)
        for i in range(7)
    ]
    q = jnp.concatenate(q, axis=1) * 0.125
    own = table[1, 0]
    for c in range(4):
        for j in range(16):
            lo, block = 128 * j, table[0, c * 16 + j]
            first = pl.ds(pl.multiple_of(block * 64, 64), 64)
            second = pl.ds(pl.multiple_of((127 - block) * 64, 64), 64)
            kv[first, :] = pieces[c][lo : lo + 64, :]
            kv[second, :] = pieces[c][lo + 64 : lo + 128, :]
    moves = [
        pltpu.make_async_copy(kv, kv_out, sems.at[0]),
        pltpu.make_async_copy(wq_ref, wq_out, sems.at[1]),
        pltpu.make_async_copy(wo_ref, wo_out, sems.at[2]),
    ]
    for move in moves:
        move.start()
    for half in range(2):
        turned = swap_heads(q[64 * half : 64 * (half + 1)])
        qt[half] = turned.astype(bf16)
        qbd[half] = two_groups(turned).astype(bf16)
        acc[half] = jnp.zeros((144, D), f32)
        top[half] = jnp.full((8, D), MASKED, f32)

    def step(half, tile, block):
        at = pl.ds(pl.multiple_of(tile * TILE, TILE), TILE)
        scores = dot(kv[at, 0:128], qbd[half])
        if block is not None:
            scores = tile_mask(scores, block, tile)
        old = top[half][0:1]
        new = jnp.maximum(old, jnp.max(scores, axis=0, keepdims=True))
        probs = jnp.exp(scores - new).astype(bf16)
        values = jnp.concatenate([kv[at, 128:256].T, jnp.ones((16, TILE), bf16)], axis=0)
        acc[half] = acc[half] * jnp.exp(old - new) + dot(values, probs)
        top[half] = jnp.broadcast_to(new, (8, D))

    over_tiles(own, step)
    halves = []
    for half in range(2):
        total = acc[half][128:129]
        out = one_group(acc[half][0:128]) / total
        ot_ref[half] = out
        lse_ref[half] = jnp.broadcast_to(top[half][0:1] + jnp.log(total), (8, D))
        halves.append(swap_heads(out))
    attended = jnp.concatenate(halves, axis=0).astype(bf16)
    att_ref[...] = attended
    middle = x[...].astype(f32) + dot(attended, wo_ref[...])
    mid_ref[...] = middle
    r = lax.rsqrt(jnp.mean(middle * middle, axis=-1, keepdims=True) + EPS)
    n2_ref[...] = (middle * r * gains[1:2, :]).astype(bf16)
    for move in moves:
        move.wait()


def attend_back_kernel(
    table, qt, wo, gains, mid, cot, gn2, ot, lse, kv, cos, sin,
    gmid_ref, gab_ref, g2_ref, gq_ref, own_ref, other_ref,
    qbd, qbt, dobd, dobt, dot_ref, dqt, dkv,
):
    own = table[1, 0]
    middle = mid[...]
    r = lax.rsqrt(jnp.mean(middle * middle, axis=-1, keepdims=True) + EPS)
    grad = gn2[...]
    scaled = grad * gains[1:2, :]
    inner = jnp.mean(scaled * middle, axis=-1, keepdims=True)
    gmid = cot[...].astype(f32) + r * (scaled - middle * r * r * inner)
    gmid_ref[...] = gmid
    g2_ref[...] = jnp.broadcast_to(jnp.sum(grad * middle * r, axis=0, keepdims=True), (8, D))
    gab = gmid.astype(bf16)
    gab_ref[...] = gab
    gatt = dot_nt(gab, wo[...]).astype(bf16).astype(f32)
    for half in range(2):
        gt = swap_heads(gatt[64 * half : 64 * (half + 1)])
        dot_ref[half] = jnp.broadcast_to(jnp.sum(gt * ot[half], axis=0, keepdims=True), (8, D))
        both = two_groups(gt)
        dobd[half] = both.astype(bf16)
        dobt[half] = both.T.astype(bf16)
        both = two_groups(qt[half].astype(f32))
        qbd[half] = both.astype(bf16)
        qbt[half] = both.T.astype(bf16)
        dqt[half] = jnp.zeros((128, D), f32)

    def clear(i, carry):
        at = pl.ds(pl.multiple_of(i * TILE, TILE), TILE)
        dkv[at, :] = jnp.zeros((TILE, 256), f32)
        return carry

    lax.fori_loop(0, SEQ // TILE, clear, 0)

    def step(half, tile, block):
        at = pl.ds(pl.multiple_of(tile * TILE, TILE), TILE)
        kt = kv[at, 0:128]
        scores = dot(kt, qbd[half])
        if block is not None:
            scores = tile_mask(scores, block, tile)
        probs = jnp.exp(scores - lse[half][0:1])
        gprobs = dot(kv[at, 128:256], dobd[half])
        dkv[at, 128:256] += dot(probs.astype(bf16), dobt[half])
        graw = (probs * (gprobs - dot_ref[half][0:1])).astype(bf16)
        dkv[at, 0:128] += dot(graw, qbt[half])
        dqt[half] += dot(kt.T, graw)

    over_tiles(own, step)
    for c in range(4):
        out = (own_ref, other_ref)[c // 2]
        for j in range(16):
            block = table[0, c * 16 + j]
            lo = (c % 2) * 2048 + 128 * j
            first = pl.ds(pl.multiple_of(block * 64, 64), 64)
            second = pl.ds(pl.multiple_of((127 - block) * 64, 64), 64)
            out[lo : lo + 64, :] = dkv[first, :].astype(bf16)
            out[lo + 64 : lo + 128, :] = dkv[second, :].astype(bf16)
    gq = jnp.concatenate(
        [swap_heads(one_group(dqt[half]) * 0.125) for half in range(2)], axis=0
    )
    c, s = cos[...], -sin[...]
    for i in range(7):
        gq_ref[:, 128 * i : 128 * (i + 1)] = rope(
            gq[:, 128 * i : 128 * (i + 1)], c, s
        ).astype(bf16)


VM = pl.BlockSpec(memory_space=pltpu.VMEM)
SM = pl.BlockSpec(memory_space=pltpu.SMEM)
ANY = pl.BlockSpec(memory_space=pl.ANY)


def params(mib):
    return pltpu.CompilerParams(vmem_limit_bytes=mib << 20)


def call(kernel, mib, outs, scratch, args, flops, moved, exps=0):
    return pl.pallas_call(
        kernel,
        out_shape=[jax.ShapeDtypeStruct(s, d) for s, d in outs],
        in_specs=[SM if a.dtype == jnp.int32 else VM for a in args],
        out_specs=[VM] * len(outs),
        scratch_shapes=scratch,
        compiler_params=params(mib),
        cost_estimate=pl.CostEstimate(
            flops=flops, bytes_accessed=moved, transcendentals=exps
        ),
    )(*args)


def pack_first(*args):
    return call(pack_first_kernel, 58, [((240, 256), bf16)], [], args, 0, 1 << 20)[0]


def packed(kernel, outs, copies, ids, *args):
    return pl.pallas_call(
        kernel,
        out_shape=[jax.ShapeDtypeStruct(s, bf16) for s in outs],
        in_specs=[SM] + [ANY] * len(args),
        out_specs=[VM] * len(outs),
        scratch_shapes=[pltpu.SemaphoreType.DMA((copies,))],
        compiler_params=params(58),
        cost_estimate=pl.CostEstimate(flops=0, bytes_accessed=6 << 20, transcendentals=0),
    )(ids, *args)


def pack_qo(*args):
    return packed(pack_qo_kernel, [(ROWS, D)], 2, *args)[0]


def pack_feed(*args):
    return packed(
        pack_feed_kernel, [(ROWS, 2 * FS), (ROWS, 2 * FS), (FS, D)], 5, *args
    )


def project(*args):
    return call(
        project_kernel,
        58,
        [((D, 256), bf16), ((8, D), f32), ((TOK, D), bf16), ((TOK, 256), bf16)],
        [],
        args,
        2 * TOK * D * 256,
        3 << 20,
    )


def attend(*args):
    outs = [
        ((SEQ, 256), bf16),
        ((2, 64, D), bf16),
        ((2, 64, D), f32),
        ((2, 8, D), f32),
        ((TOK, D), bf16),
        ((TOK, D), f32),
        ((TOK, D), bf16),
        ((D, D), bf16),
        ((D, D), bf16),
    ]
    return pl.pallas_call(
        attend_kernel,
        out_shape=[jax.ShapeDtypeStruct(s, d) for s, d in outs],
        in_specs=[SM if a.dtype == jnp.int32 else VM for a in args],
        out_specs=[ANY] + [VM] * 6 + [ANY] * 2,
        scratch_shapes=[
            pltpu.VMEM((2, 128, D), bf16),
            pltpu.VMEM((2, 144, D), f32),
            pltpu.VMEM((2, 8, D), f32),
            pltpu.VMEM((SEQ, 256), bf16),
            pltpu.VMEM((D, D), bf16),
            pltpu.VMEM((D, D), bf16),
            pltpu.SemaphoreType.DMA((3,)),
        ],
        compiler_params=params(58),
        cost_estimate=pl.CostEstimate(
            flops=20_000_000_000, bytes_accessed=12 << 20, transcendentals=17 * TILE * D
        ),
    )(*args)


def attend_back(*args):
    return call(
        attend_back_kernel,
        58,
        [
            ((TOK, D), f32),
            ((TOK, D), bf16),
            ((8, D), f32),
            ((TOK, D), bf16),
            ((SEQ // 2, 256), bf16),
            ((SEQ // 2, 256), bf16),
        ],
        [
            pltpu.VMEM((2, 128, D), bf16),
            pltpu.VMEM((2, D, 128), bf16),
            pltpu.VMEM((2, 128, D), bf16),
            pltpu.VMEM((2, D, 128), bf16),
            pltpu.VMEM((2, 8, D), f32),
            pltpu.VMEM((2, 128, D), f32),
            pltpu.VMEM((SEQ, 256), f32),
        ],
        args,
        38_000_000_000,
        16 << 20,
        17 * TILE * D,
    )


def feed_kernel(ids, n0, n1, n2, n3, cots, gu_own, gu_got, down, ga, gb, ggu, hid, cot, gu):
    wt = ids[0]
    gu[pl.ds(pl.multiple_of(wt * ROWS, 64), ROWS), :] = gu_own[...]
    gu[pl.ds(pl.multiple_of((1 - wt) * ROWS, 64), ROWS), :] = gu_got[...]
    for tile, n in enumerate((n0, n1, n2, n3)):
        order = (GRAY_AB, GRAY_BA)[tile % 2]
        for p in range(4):
            index = (ids[1] ^ order[p]) * 2 + (ids[4] ^ (tile // 2))
            at = 64 * (tile % 2)
            cot[tile, 64 * p : 64 * (p + 1), :] = cots[index, at : at + 64, :]
        half, rows = tile // 2, slice(256 * (tile % 2), 256 * (tile % 2) + 256)
        pre = dot(n[...], gu[...])
        gate, up = pre[:, :FS], pre[:, FS:]
        ghidden = dot_nt(cot[tile], down[...])
        sigmoid = 1.0 / (1.0 + jnp.exp(-gate))
        swish = gate * sigmoid
        hid[half, rows, :] = (swish * up).astype(bf16)
        ggate = ghidden * up * sigmoid * (1.0 + gate * (1.0 - sigmoid))
        ggu[half, rows, 0:FS] = ggate.astype(bf16)
        ggu[half, rows, FS:] = (ghidden * swish).astype(bf16)
        (ga, gb)[half][rows, :] = dot_nt(ggu[half, rows, :], gu[...]).astype(bf16)


def feed(*args):
    return call(
        feed_kernel,
        32,
        [
            ((512, D), bf16),
            ((512, D), bf16),
            ((2, 512, 2 * FS), bf16),
            ((2, 512, FS), bf16),
            ((4, 256, D), bf16),
        ],
        [pltpu.VMEM((D, 2 * FS), bf16)],
        args,
        2 * 1024 * D * 5 * FS,
        15 << 20,
    )


def down_side_kernel(hid, cot, down, la, lb, dn):
    for half, out in ((0, la), (1, lb)):
        both = dot(hid[half], down[...]).astype(bf16)
        for p in range(4):
            q = GRAY_BA.index(GRAY_AB[p])
            out[p, 0:64, :] = both[64 * p : 64 * (p + 1)]
            out[p, 64:128, :] = both[256 + 64 * q : 256 + 64 * (q + 1)]
    total = dot(hid[0, 0:256, :].T, cot[0]) + dot(hid[0, 256:512, :].T, cot[1])
    total += dot(hid[1, 0:256, :].T, cot[2]) + dot(hid[1, 256:512, :].T, cot[3])
    dn[...] = total


def down_side(*args):
    return call(
        down_side_kernel,
        24,
        [((4, TOK, D), bf16), ((4, TOK, D), bf16), ((FS, D), f32)],
        [],
        args,
        4 * 1024 * D * FS,
        8 << 20,
    )


def feed_grads_kernel(ids, n0, n1, n2, n3, ggu, dn, *rest):
    outs, gu = rest[:8], rest[8]
    z, x = ids[2], ids[3]
    nat = jnp.concatenate([n0[...].T, n1[...].T], axis=1)
    nbt = jnp.concatenate([n2[...].T, n3[...].T], axis=1)
    for h in range(2):
        rows = slice(h * ROWS, (h + 1) * ROWS)
        for j in range(2):
            at = slice(j * FS, (j + 1) * FS)
            both = dot(nat[rows], ggu[0, :, at]) + dot(nbt[rows], ggu[1, :, at])
            gu[h, 0:ROWS, at] = both.astype(bf16)
        gu[h, ROWS:512, :] = jnp.zeros((64, 2 * FS), bf16)
    for zi in range(4):
        for xi in range(4):
            vz, vx = GRAY_AB[zi], GRAY_AB[xi]
            i = (z ^ vz) * 4 + (x ^ vx)
            rows = pl.ds(pl.multiple_of(i * 32, 32), 32)
            low = pl.ds(pl.multiple_of(i * 32, 32), 16)
            high = pl.ds(pl.multiple_of(i * 32 + 16, 16), 16)
            extra = dn[pl.ds(pl.multiple_of(512 + i * 8, 8), 8), :]
            extra = jnp.concatenate(
                [
                    extra[:, 0:384],
                    extra[:, 384:768],
                    jnp.concatenate([extra[:, 768:896], jnp.zeros((8, 256), f32)], axis=1),
                    jnp.zeros((8, 384), f32),
                ],
                axis=0,
            )
            half = zi // 2
            p = (xi, GRAY_BA.index(vx))[half]
            a = outs[2 * half + p // 2]
            a[p % 2, zi % 2, 0:32, :] = gu[0, rows, :]
            a[p % 2, zi % 2, 32:48, :] = gu[1, low, :]
            half = xi // 2
            q = (zi, GRAY_BA.index(vz))[half]
            b = outs[4 + 2 * half + q // 2]
            b[q % 2, xi % 2, 0:16, :] = gu[1, high, :]
            b[q % 2, xi % 2, 16:48, 0:896] = dn[rows, :].astype(bf16)
            b[q % 2, xi % 2, 16:48, 896:] = extra.astype(bf16)


def feed_grads(*args):
    return call(
        feed_grads_kernel,
        28,
        [((2, 2, 48, 2 * FS), bf16)] * 8,
        [pltpu.VMEM((2, 512, 2 * FS), bf16)],
        args,
        2 * 1024 * D * 2 * FS,
        14 << 20,
    )


def place_ab(v):
    return v ^ (v >> 1)


def finish_kernel(source, ids, feed, *rest):
    gate, up, down = rest[-6:-3]
    wide, tall, sems = rest[-3:]
    src = ids[4] if source == 0 else 1 - ids[4]
    moves = []
    for ylo in range(2):
        member = ylo * 2 + src
        for wt in range(2):
            at = pl.multiple_of(wt * FHALF + member * FS, 128)
            for m, out in ((0, gate), (1, up)):
                k = (ylo * 2 + wt) * 2 + m
                lanes = slice(m * FS, (m + 1) * FS)
                for i in range(14):
                    part = feed[i, ylo, 32 * wt : 32 * wt + 32, lanes]
                    wide[k, 32 * i : 32 * i + 32, :] = part.astype(f32)
                moves.append((ylo, src, wide.at[k], out, at, sems.at[k], False))
                push(*moves[-1], True)
        for i in range(16):
            tall[ylo, 32 * i : 32 * i + 32, :] = feed[i, ylo, 64:96, 0:896].astype(f32)
            extra = feed[i, ylo, 64:96, 896:].astype(f32)
            rows = slice(512 + 8 * i, 520 + 8 * i)
            tall[ylo, rows, 0:384] = extra[0:8]
            tall[ylo, rows, 384:768] = extra[8:16]
            tall[ylo, rows, 768:896] = extra[16:24, 0:128]
        at = pl.multiple_of(member * FS, 128)
        moves.append((ylo, src, tall.at[ylo], down, at, sems.at[8 + ylo], True))
        push(*moves[-1], True)
    for move in moves:
        push(*move, False)


def push(ylo, src, buffer, out, at, sem, tall, begin):
    def go(size):
        if tall:
            copy = pltpu.make_async_copy(
                buffer.at[0:size, :], out.at[pl.ds(at, size), :], sem
            )
        else:
            copy = pltpu.make_async_copy(
                buffer.at[:, 0:size], out.at[:, pl.ds(at, size)], sem
            )
        if begin:
            copy.start()
        else:
            copy.wait()

    if ylo == 0:
        go(FS)
    else:

        @pl.when(src == 0)
        def _():
            go(FS)

        @pl.when(src == 1)
        def _():
            go(512)


def finish(source, ids, feed, outs):
    shapes = [(ROWS, FF), (ROWS, FF), (FHALF, D)]
    return pl.pallas_call(
        functools.partial(finish_kernel, source),
        out_shape=[jax.ShapeDtypeStruct(s, f32) for s in shapes],
        in_specs=[SM, VM] + [ANY] * len(outs),
        out_specs=[ANY] * 3,
        scratch_shapes=[
            pltpu.VMEM((8, ROWS, FS), f32),
            pltpu.VMEM((2, FS, D), f32),
            pltpu.SemaphoreType.DMA((10,)),
        ],
        input_output_aliases={2: 0, 3: 1, 4: 2} if outs else {},
        compiler_params=params(58),
        cost_estimate=pl.CostEstimate(flops=0, bytes_accessed=22 << 20, transcendentals=0),
    )(ids, feed, *outs)


def pad_rows(rows, count, width):
    return jnp.concatenate(
        rows + [jnp.zeros((count - len(rows), width), f32)], axis=0
    )


def proj_grads_kernel(ids, att, gab, n1, gq, g2, la, lb, keep, send, o, q):
    o[...] = dot(att[...].T, gab[...]).astype(bf16)
    q[...] = dot(n1[...].T, gq[...]).astype(bf16)
    sums = jnp.sum(gq[...].astype(f32), axis=0, keepdims=True)
    o_rows = pad_rows([g2[0:1, :]], 16, D).astype(bf16)
    q_rows = pad_rows([sums], 16, D).astype(bf16)
    for c, out, lout in ((0, keep, la), (1, send, lb)):
        for half, (full, extra) in enumerate(((o, o_rows), (q, q_rows))):
            for p in range(4):
                v = (GRAY_AB, GRAY_BA)[half][p]
                m = (ids[1] ^ v) * 2 + (ids[4] ^ c)
                out[half, p, 0:112, :] = full[pl.ds(pl.multiple_of(m * 112, 16), 112), :]
                out[half, p, 112:128, :] = extra
                at = 64 * half
                out[half, p, 128:192, :] = lout[GRAY_AB.index(v), at : at + 64, :]


def proj_grads(*args):
    return call(
        proj_grads_kernel,
        24,
        [((2, 4, 192, D), bf16)] * 2,
        [pltpu.VMEM((D, D), bf16), pltpu.VMEM((D, D), bf16)],
        args,
        4 * TOK * D * D,
        6 << 20,
    )


def kv_grads_kernel(ids, table, dkv, n1, speed, keep, send, all_n1, both):
    row = lax.broadcasted_iota(jnp.int32, (64, 128), 0)
    inner = row.astype(f32) * speed[...]
    cos_in, sin_in = jnp.cos(inner), jnp.sin(inner)
    row = lax.broadcasted_iota(jnp.int32, (16, 128), 0)
    start = jnp.zeros((16, 128), f32)
    for j in range(8):
        block = table[2, j]
        start = jnp.where(row == 2 * j, (block * 64).astype(f32), start)
        start = jnp.where(row == 2 * j + 1, ((127 - block) * 64).astype(f32), start)
    outer = start * speed[...]
    cos_out, sin_out = jnp.cos(outer), jnp.sin(outer)
    lane = lax.broadcasted_iota(jnp.int32, (64, 128), 1)
    sign = jnp.where(lane % 64 < 32, 1.0, -1.0)
    for j in range(16):
        c, s = cos_out[j : j + 1], sin_out[j : j + 1]
        cosine = cos_in * c - sin_in * s
        sine = (sin_in * c + cos_in * s) * sign
        rows = slice(64 * j, 64 * (j + 1))
        both[rows, 0:128] = rope(dkv[rows, 0:128].astype(f32), cosine, sine).astype(bf16)
    both[:, 128:256] = dkv[:, 128:256]
    for p in range(4):
        for a in range(2):
            index = ((ids[1] & 1) ^ a) * 4 + ((ids[3] - p) & 3)
            at = (2 * p + a) * TOK
            all_n1[at : at + TOK, :] = n1[index]
    wide = dot(all_n1[...].T, both[...]).astype(bf16)
    sums = jnp.sum(both[...].astype(f32), axis=0, keepdims=True)
    sums = pad_rows([sums], 16, 256).astype(bf16)
    for m in range(8):
        s = (m // 2 - ids[1]) & 3
        rows = wide[112 * m : 112 * (m + 1)]

        @pl.when(m % 2 == ids[4])
        def _():
            keep[s, 0:112, :] = rows
            keep[s, 112:128, :] = sums

        @pl.when(m % 2 != ids[4])
        def _():
            send[s, 0:112, :] = rows
            send[s, 112:128, :] = sums


def kv_grads(*args):
    return call(
        kv_grads_kernel,
        20,
        [((4, TOK, 256), bf16)] * 2,
        [pltpu.VMEM((1024, D), bf16), pltpu.VMEM((1024, 256), bf16)],
        args,
        2 * 1024 * D * 256,
        4 << 20,
    )


def last_kernel(ids, g0, g1, gq, wq, wkv, tok, gains, gmid, cos, sin, grad_ref):
    both = g0[...].astype(f32) + g1[...].astype(f32)
    key = rope(both[:, 0:128], cos[...], -sin[...]).astype(bf16)
    both = jnp.concatenate([key, both[:, 128:256].astype(bf16)], axis=1)
    gn1 = dot_nt(gq[...], wq[...]) + dot_nt(both, wkv[...])
    x = tok[...].astype(f32)
    r = lax.rsqrt(jnp.mean(x * x, axis=-1, keepdims=True) + EPS)
    scaled = gn1 * gains[0:1, :]
    inner = jnp.mean(scaled * x, axis=-1, keepdims=True)
    grad_ref[...] = gmid[...] + r * (scaled - x * r * r * inner)


def last(*args):
    return call(
        last_kernel,
        16,
        [((TOK, D), f32)],
        [],
        args,
        4 * TOK * D * 1152,
        5 << 20,
    )[0]


YL = ("wt", "ylo")
ALL = ("wt", "ylo", "z", "x", "core")
together = lax.optimization_barrier


def pair(a, axis):
    return lax.ppermute(a, axis, [(0, 1), (1, 0)])


def near(a, axis, v):
    return lax.ppermute(a, axis, [(i, i ^ v) for i in range(4)])


def in_order(first, mine, other):
    return jnp.where(
        first, jnp.concatenate([mine, other], 0), jnp.concatenate([other, mine], 0)
    )


def total_of(*parts):
    total = parts[0].astype(f32)
    for p in parts[1:]:
        total += p.astype(f32)
    return total.astype(bf16)


def grow(a, axis, order):
    for v in order:
        a = jnp.concatenate([a, near(a, axis, v)], 0)
    return a


def shrink(a, axis, order):
    for v in order[::-1]:
        half = a.shape[0] // 2
        a = total_of(a[:half], near(a[half:], axis, v))
    return a


def ring_parts(a, axis):
    return [a] + [shift(a, axis, s) for s in (1, 2, 3)]


def after(a, dep):
    return together((a, dep))[0]


def per_device(
    tokens,
    cotangent,
    block_pair,
    first_gain,
    query_weight,
    query_bias,
    key_weight,
    key_bias,
    value_weight,
    value_bias,
    output_weight,
    second_gain,
    gate_weight,
    up_weight,
    down_weight,
):
    wt, ylo, z, x, core = (lax.axis_index(a).astype(jnp.int32) for a in ALL)
    first_wt = wt == 0
    member = ylo * 2 + core
    ids = jnp.stack([wt, wt * 2 + ylo, z, x, core, member, wt, wt])
    token = tokens[0]
    cot = cotangent[0]

    small = (first_gain, second_gain, query_bias, key_bias, value_bias)
    packed = pack_first(ids, key_weight, value_weight, *small)
    got = pair(packed, "wt")
    got2 = pair(got, "core")
    cots = lax.all_gather(cot, ("wt", "ylo", "core"))

    pairs = block_pair[0]
    here = ((ylo * 4 + z) * 4 + x) * 2 + core
    own = lax.dynamic_index_in_dim(pairs, here, 0, keepdims=False)
    r2 = jnp.arange(2, dtype=jnp.int32)
    of_core = (core ^ r2)[:, None, None, None, None]
    of_z = (z ^ jnp.array([GRAY_AB, GRAY_BA], jnp.int32))[None, :, :, None, None]
    of_x = ((x - jnp.array([[0, 1], [2, 3]], jnp.int32)) & 3)[None, :, None, :, None]
    of_y = (ylo ^ r2)[None, None, None, None, :]
    slots = (((of_y * 4 + of_z) * 4 + of_x) * 2 + of_core).reshape(-1)
    around = (((ylo ^ r2)[None, :] * 4 + z) * 4 + ((x - jnp.arange(4, dtype=jnp.int32)) & 3)[:, None]) * 2
    around = jnp.pad((around + core).reshape(-1), (0, 56))
    found = pairs[jnp.concatenate([slots, around])].reshape(2, 64)
    table = jnp.stack([found[0], jnp.broadcast_to(own, (64,)), found[1]]).astype(jnp.int32)

    offsets = jnp.arange(64, dtype=jnp.int32)
    inverse = THETA ** (-(2.0 * jnp.arange(32, dtype=f32)) / HD)

    places = jnp.concatenate([own * 64 + offsets, (127 - own) * 64 + offsets])
    angle = places.astype(f32)[:, None] * inverse[None, :]
    c, s = jnp.cos(angle), jnp.sin(angle)
    cosine = jnp.concatenate([c, c, c, c], 1)
    sine = jnp.concatenate([-s, s, -s, s], 1)
    speed = jnp.concatenate([inverse] * 4)[None]

    wkv, gains, n1, kv = project(
        ids, token, key_weight, value_weight, *small, got, got2, cosine, sine
    )
    qo_send = pack_qo(after(ids, kv), output_weight, query_weight)
    kv_got = pair(kv, "ylo")
    kv_got, qo_send = together((kv_got, qo_send))
    qo_got = pair(qo_send, "wt")
    qo_got2 = pair(qo_got, "core")
    kv = jnp.concatenate([kv, kv_got], 0)
    parts = ring_parts(kv, "x")
    lo = jnp.concatenate(parts[:2], 0)
    hi = jnp.concatenate(parts[2:], 0)
    lo, hi = together((lo, hi))
    lo, hi = grow(lo, "z", (1,)), grow(hi, "z", (3,))
    lo, hi, table = together((lo, hi, table))
    gu_send, gu_own, down = pack_feed(after(ids, lo), gate_weight, up_weight, down_weight)
    lo, hi = grow(lo, "z", (3,)), grow(hi, "z", (1,))
    lo, hi, gu_send, qo_got2 = together((lo, hi, gu_send, qo_got2))
    gu_got = pair(gu_send, "wt")
    pieces = [lo, hi, pair(lo, "core"), pair(hi, "core")]

    kv, qt, ot, lse, attended, middle, n2, query_mat, output_mat = attend(
        ids, table, n1, query_weight, output_weight, qo_got, qo_got2, cosine, sine,
        token, gains, *pieces,
    )

    tiles = [grow(n2[:64], YL, (1,)), grow(n2[64:], YL, (3,))]
    tiles, gu_got, cots = together((tiles, gu_got, cots))
    tiles = [grow(tiles[0], YL, (3,)), grow(tiles[1], YL, (1,))]
    tiles = tiles + [pair(a, "core") for a in tiles]
    gn2_own, gn2_other, ggu, hidden, cots = feed(ids, *tiles, cots, gu_own, gu_got, down)
    lout_own, lout_other, dn_grad = down_side(hidden, cots, down)
    gn2 = total_of(gn2_own, pair(gn2_other, "core"))
    grads = feed_grads(ids, *tiles, ggu, dn_grad)
    gn2, grads = together((gn2, grads))
    gn2 = jnp.concatenate([shrink(gn2[:256], YL, AB), shrink(gn2[256:], YL, BA)], 0)
    ways = (("x", 3, 1), ("x", 1, 3), ("z", 3, 1), ("z", 1, 3))
    first = [near(grads[2 * i + 1], a, v) for i, (a, v, u) in enumerate(ways)]
    first = together(first)
    second = [
        near(total_of(grads[2 * i][1], first[i][1]), a, u) for i, (a, v, u) in enumerate(ways)
    ]

    gmid, gab, g2, gq, dkv, dkv_other = attend_back(
        table, qt, output_mat, gains, middle, cot, gn2.astype(f32), ot, lse, kv, cosine, sine
    )
    n1_all = lax.all_gather(after(n1, first), ("ylo", "x"))
    gq, gab, g2, dkv, dkv_other, second, n1_all = together(
        (gq, gab, g2, dkv, dkv_other, second, n1_all)
    )

    dkv = total_of(dkv, pair(dkv_other, "core"))
    sums = [total_of(grads[2 * i][0], first[i][0], second[i]) for i in range(4)]
    part_a = total_of(sums[0], near(sums[1], "z", 3))
    part_b = total_of(sums[2], near(sums[3], "x", 3))
    keep, send = proj_grads(ids, attended, gab, n1, gq, g2, lout_own, lout_other)
    dkv, part_a, part_b, keep, send = together((dkv, part_a, part_b, keep, send))

    lo, hi = shrink(dkv[:2048], "z", (3,)), shrink(dkv[2048:], "z", (1,))
    part_a, part_b = shrink(part_a, "z", (1,))[0], shrink(part_b, "x", (1,))[0]
    send = pair(send, "core")
    lower = part_a[0:32]
    upper = jnp.concatenate([part_a[32:48], part_b[0:16]], 0)
    ours = jnp.where(first_wt, lower, upper)
    theirs = jnp.where(first_wt, upper, lower)
    ours = jnp.concatenate([ours, part_b[16:48]], 0)
    swapped, ours_y, swapped_y = near(theirs, YL, 2), near(ours, YL, 1), near(theirs, YL, 3)
    row_own = jnp.concatenate([in_order(first_wt, ours[:32], swapped), ours[32:]], 0)
    row_far = jnp.concatenate([in_order(first_wt, ours_y[:32], swapped_y), ours_y[32:]], 0)
    mine = in_order(ylo == 0, row_own[None], row_far[None])
    lo, hi, keep, send, mine = together((lo, hi, keep, send, mine))

    feed_own = lax.all_gather(mine, ("z", "x"))
    lo, hi = shrink(lo, "z", (1,)), shrink(hi, "z", (3,))
    part = total_of(keep, send)
    o_part, q_part = shrink(part[0], YL, (3,)), shrink(part[1], YL, (1,))
    dkv = jnp.concatenate([lo, hi], 0)
    dkv, o_part, q_part = together((dkv, o_part, q_part))

    kv_keep, kv_send = kv_grads(ids, table, dkv, n1_all, speed)
    kv = total_of(kv_keep, pair(kv_send, "core"))
    parts = [dkv[256 * s : 256 * (s + 1)] for s in range(4)]
    dkv = total_of(parts[0], *[shift(parts[s], "x", 4 - s) for s in (1, 2, 3)])
    o_part, q_part = shrink(o_part, YL, (1,))[0], shrink(q_part, YL, (3,))[0]
    dkv, kv, o_part, q_part = together((dkv, kv, o_part, q_part))

    kv = total_of(kv[0], *[shift(kv[s], YL, s) for s in (1, 2, 3)])
    dkv_got = pair(dkv[TOK:], "ylo")
    dkv_got, kv = together((dkv_got, kv))

    lout = jnp.concatenate([o_part[128:], q_part[128:]], 0)
    layer_out = (middle + lout.astype(f32)).astype(bf16)[None]
    whole = jnp.concatenate([o_part[:128], q_part[:128], kv], 1)

    def strip(s):
        return lax.dynamic_slice_in_dim(whole, ((z + s) & 3) * 32, 32, 0)

    input_grad = last(
        ids, dkv[:TOK], dkv_got, gq, query_mat, wkv, token, gains, gmid, cosine, sine
    )
    whole = total_of(strip(0), *[shift(strip(s), "z", s) for s in (1, 2, 3)])
    whole, input_grad = together((whole, input_grad))

    whole = total_of(*ring_parts(whole, "x"))
    whole, feed_own = together((whole, feed_own))
    feed_other = pair(feed_own, "core")
    outs = finish(0, ids, feed_own, [])

    strips = [whole] + [shift(whole, "z", s) for s in (1, 2, 3)]
    whole = jnp.zeros((4, 32, 2048), bf16)
    for s in range(4):
        whole = lax.dynamic_update_slice_in_dim(whole, strips[s][None], (z - s) & 3, 0)
    whole = whole.reshape(1, 128, 2048)
    whole, outs = together((whole, outs))
    sums = whole[0, 112].astype(f32)
    other, outs = together((pair(whole, "ylo"), finish(1, ids, feed_other, outs)))
    gate_grad, up_grad, down_grad = outs
    whole = in_order(ylo == 0, whole, other)[:, None]
    far = pair(whole, "core")
    whole = jnp.where(
        core == 0, jnp.concatenate([whole, far], 1), jnp.concatenate([far, whole], 1)
    )

    def rows(at, width):
        return whole[:, :, :112, at : at + width].reshape(ROWS, width).astype(f32)

    def slice_of(a, size):
        return lax.dynamic_slice_in_dim(a, wt * size, size, 0)

    query_grad = rows(D, D)
    key_grad, value_grad = rows(2 * D, 128), rows(2 * D + 128, 128)
    gain_grad = jnp.sum(query_grad * query_weight.astype(f32), 1)
    gain_grad += jnp.sum(key_grad * key_weight.astype(f32), 1)
    gain_grad += jnp.sum(value_grad * value_weight.astype(f32), 1)
    return (
        layer_out,
        input_grad[None],
        gain_grad / first_gain.astype(f32),
        query_grad,
        slice_of(sums[D : 2 * D], ROWS),
        key_grad,
        slice_of(sums[2 * D : 2 * D + 128], 64),
        value_grad,
        slice_of(sums[2 * D + 128 :], 64),
        rows(0, D),
        slice_of(sums[:D], ROWS),
        gate_grad,
        up_grad,
        down_grad,
    )


def solution(mesh):
    fine = Mesh(mesh.devices.reshape(2, 2, 4, 4, 2), ALL)
    ctx = ("ylo", "z", "x", "core")
    rows, mats = P("wt"), P("wt", None)
    whole = P("wt", ctx, None)
    return jax.shard_map(
        per_device,
        mesh=fine,
        in_specs=(
            whole, whole, mats, rows, mats, rows, mats, rows, mats, rows,
            mats, rows, mats, mats, mats,
        ),
        out_specs=(
            whole, whole, rows, mats, rows, mats, rows, mats, rows, mats,
            rows, mats, mats, mats,
        ),
        check_vma=False,
    )
```
